32 devices in a mesh: leaf: 8 (over z, y), rep: 4 (over x, core).
Axes of the slice: x: 2, y: 2, z: 4, core: 2. Of those that a mesh axis runs over, the one named last changes fastest.
Arguments:
- fine_moments: bfloat16 [128, 8, 8, 152], P('leaf'), may hold values from -6 to 6
- fine_present: int32 [128, 8, 8], P('leaf'), may hold values 0 or 1
- coarse_moments: bfloat16 [64, 4, 4, 152], P('leaf'), may hold values from -6 to 6
- coarse_present: int32 [64, 4, 4], P('leaf'), may hold values 0 or 1
- coarse_incoming: float32 [64, 4, 4, 152], P('leaf'), may hold values from -6 to 6
- check_to_density: float32 [152, 152], replicated, may hold values from -0.5 to 0.5
Outputs:
- fine_density: float32 [8, 64, 4, 4, 152], P('rep', 'leaf')
The draws below stay inside these ranges and needn't reach their ends.
All inputs are finite; a program needn't handle non-finite values. No bound on the sum of `fine_present` or of `coarse_present` on one device may be relied on, other than what follows from the above.
Results may differ from the reference program's by a relative error of at most 0.0003.
The reference program's roundings to bfloat16 on the way count: a program that leaves them out, or rounds other values in their place, can miss the bound.
Values may be sent and summed in bfloat16 or wider, within the bound.
A program may use at most 64 MiB of HBM per device.

```python
import jax
import jax.numpy as jnp
import numpy as np
from jax import lax

ORDER = 6
COEFFS = 152
SIDE = 8
DEPTH = 128
HALF_DEPTH = 64
HALF_SIDE = 4


def set_ends(drawn, own_key, low, largest):
    place = [jax.random.randint(jax.random.fold_in(own_key, axis), (), 0, length) for axis, length in enumerate(drawn.shape)]
    longest = drawn.shape.index(max(drawn.shape))
    neighbour = place[:longest] + [(place[longest] + 1) % drawn.shape[longest]] + place[longest + 1:]
    return drawn.at[tuple(place)].set(low).at[tuple(neighbour)].set(largest)


def block_levels(key, shape, cuts, smallest, top_value):
    gain = 1.0
    for dim, parts in cuts:
        draws = jax.random.uniform(jax.random.fold_in(jax.random.fold_in(key, 6), dim), (parts,), jnp.float32, smallest / len(cuts), top_value / len(cuts))
        gain = gain * jnp.repeat(jnp.exp(draws), shape[dim] // parts).reshape((-1,) + (1,) * (len(shape) - 1 - dim))
    return gain


def scatter_about(key, shape, deviation, limit, split=(), kind=jnp.bfloat16):
    drawn = deviation * jax.random.normal(key, shape, jnp.float32)
    if split:
        drawn = drawn * block_levels(key, shape, split, -0.22, 0.18)
    return jnp.clip(drawn, -limit, limit).astype(kind)


def setup_inputs(seed: int = 0) -> dict:
    keys = jax.random.split(jax.random.key(seed), 7)
    return {
        "fine_moments": scatter_about(keys[0], (DEPTH, SIDE, SIDE, COEFFS), 1.0, 6.0, ((0, 8),)),
        "fine_present": set_ends((jax.random.randint(keys[1], (DEPTH, SIDE, SIDE), 0, 4) < 3).astype(jnp.int32), jax.random.fold_in(keys[1], 1), 0, 1),
        "coarse_moments": scatter_about(keys[2], (HALF_DEPTH, HALF_SIDE, HALF_SIDE, COEFFS), 1.0, 6.0, ((0, 8),)),
        "coarse_present": set_ends((jax.random.randint(keys[3], (HALF_DEPTH, HALF_SIDE, HALF_SIDE), 0, 8) < 7).astype(jnp.int32), jax.random.fold_in(keys[3], 1), 0, 1),
        "coarse_incoming": scatter_about(keys[4], (HALF_DEPTH, HALF_SIDE, HALF_SIDE, COEFFS), 1.0, 6.0, ((0, 8),), jnp.float32),
        "check_to_density": scatter_about(keys[5], (COEFFS, COEFFS), COEFFS ** -0.5, 0.5, (), jnp.float32),
    }


strength = 0.04

def surface_points(order):
    chosen = []
    for height in range(order):
        for across in range(order):
            for along in range(order):
                on_edge = [coordinate in (0, order - 1) for coordinate in (height, across, along)]
                if any(on_edge):
                    chosen.append((height, across, along))
    return np.array(chosen, np.int32)

def surface_coordinates():
    lattice = jnp.asarray(surface_points(ORDER), jnp.int32).astype(jnp.float32)
    return lattice * (2.0 / (ORDER - 1)) - 1.0

def octant_bit_table():
    return np.array([[octant >> 2 & 1, octant >> 1 & 1, octant & 1] for octant in range(8)], np.int32)

def interaction_table():
    entries = np.zeros((8, 192, 4), np.int32)
    entries[:, :, :3] = 3
    for octant in range(8):
        parity = octant_bit_table()[octant]
        found = []
        for vertical in range(-2 - parity[0], 4 - parity[0]):
            for lateral in range(-2 - parity[1], 4 - parity[1]):
                for forward in range(-2 - parity[2], 4 - parity[2]):
                    if max(abs(vertical), abs(lateral), abs(forward)) >= 2:
                        found.append((vertical, lateral, forward))
        entries[octant, :len(found), :3] = np.array(found, np.int32)
        entries[octant, :len(found), 3] = 1
    return entries

def translation_ops(offsets, valid):
    surface = surface_coordinates()
    gaps = []
    for axis_index in range(3):
        target = 0.525 * surface[:, axis_index]
        source = 0.525 * surface[None, :, axis_index] + offsets[:, axis_index].astype(jnp.float32)[:, None]
        gaps.append(target[None, None, :] - source[:, :, None])
    squared = gaps[0] ** 2 + gaps[1] ** 2 + gaps[2] ** 2
    return (strength * valid[:, None, None] / jnp.sqrt(squared)).astype(jnp.bfloat16)

def transfer_ops(octant_bits):
    surface = surface_coordinates()
    gaps = []
    for axis_index in range(3):
        child = octant_bits[:, axis_index].astype(jnp.float32)[:, None] - 0.5 + 0.525 * surface[None, :, axis_index]
        parent = 2.95 * surface[:, axis_index]
        gaps.append(child[:, None, :] - parent[None, :, None])
    squared = gaps[0] ** 2 + gaps[1] ** 2 + gaps[2] ** 2
    return (strength / jnp.sqrt(squared)).astype(jnp.bfloat16)

def parity_stack(padded):
    dims = padded.shape
    shaped = padded.reshape(dims[0] // 2, 2, dims[1] // 2, 2, dims[2] // 2, 2, dims[3])
    return shaped.transpose(1, 3, 5, 0, 2, 4, 6).reshape(8, dims[0] // 2, dims[1] // 2, dims[2] // 2, dims[3])

def strided_cut(stacked, corner, extent):
    parity = corner % 2
    selected = parity[0] * 4 + parity[1] * 2 + parity[2]
    starts = corner // 2
    nought = jnp.zeros((), jnp.int32)
    window = lax.dynamic_slice(stacked, (selected, starts[0], starts[1], starts[2], nought), (1, extent[0] // 2, extent[1] // 2, extent[2] // 2, stacked.shape[4]))
    return window.reshape(-1, stacked.shape[4])

def octant_layout(field):
    halves = (field.shape[0] // 2, field.shape[1] // 2, field.shape[2] // 2)
    trailing = field.shape[3:]
    shaped = field.reshape((halves[0], 2, halves[1], 2, halves[2], 2) + trailing)
    moved = shaped.transpose((1, 3, 5, 0, 2, 4) + tuple(range(6, 6 + len(trailing))))
    return moved.reshape((8, halves[0] * halves[1] * halves[2]) + trailing)

def natural_layout(grouped, extent):
    feature = grouped.shape[2]
    shaped = grouped.reshape(2, 2, 2, extent[0] // 2, extent[1] // 2, extent[2] // 2, feature)
    return shaped.transpose(3, 0, 4, 1, 5, 2, 6).reshape(extent[0], extent[1], extent[2], feature)

def density(check, check_to_density, present_rows, factor):
    mapped = jnp.einsum('nrk,kl->nrl', check, check_to_density, precision=lax.Precision.HIGHEST, preferred_element_type=jnp.float32)
    return factor * mapped * present_rows[..., None]

def level_checks(moments, present, factor):
    feature = moments.shape[3]
    extent = moments.shape[:3]
    masked = moments * present[..., None].astype(jnp.bfloat16)
    stacked = parity_stack(jnp.pad(masked, ((3, 3), (3, 3), (3, 3), (0, 0))))
    offsets_table = jnp.asarray(interaction_table())
    cell_count = extent[0] * extent[1] * extent[2] // 8
    results = []
    for octant in range(8):
        octant_bits = jnp.asarray(octant_bit_table()[octant])

        def visit(running, entry):
            corner = octant_bits + entry[:3] + 3
            weight = translation_ops(entry[None, :3], entry[None, 3].astype(jnp.float32))[0] * factor
            pieces = strided_cut(stacked, corner, extent)
            return (running + jnp.dot(pieces, weight, preferred_element_type=jnp.float32), None)
        running, _ = lax.scan(visit, jnp.zeros((cell_count, feature), jnp.float32), offsets_table[octant])
        results.append(running)
    return jnp.stack(results)

def reference(fine_moments, fine_present, coarse_moments, coarse_present, coarse_incoming, check_to_density):
    feature = fine_moments.shape[3]
    coarse_check = level_checks(coarse_moments, coarse_present, 0.5) + octant_layout(coarse_incoming)
    coarse_density = density(coarse_check, check_to_density, octant_layout(coarse_present).astype(jnp.float32), 2.0).astype(jnp.bfloat16)
    parents = natural_layout(coarse_density, coarse_moments.shape[:3]).reshape(-1, feature)
    fine_check = level_checks(fine_moments, fine_present, 1.0)
    transfer = transfer_ops(jnp.asarray(octant_bit_table()))
    fine_check = fine_check + jnp.einsum('rk,nkl->nrl', parents.astype(jnp.float32), transfer.astype(jnp.float32), precision=lax.Precision.HIGHEST)
    fine_density = density(fine_check, check_to_density, octant_layout(fine_present).astype(jnp.float32), 1.0)
    extent = fine_moments.shape[:3]
    return fine_density.reshape(8, extent[0] // 2, extent[1] // 2, extent[2] // 2, feature)
```

```python
import functools

import jax
import jax.numpy as jnp
import ml_dtypes
import numpy as np
from jax import lax
from jax.experimental import pallas as pl
from jax.experimental.pallas import tpu as pltpu
from jax.sharding import PartitionSpec as P

ORDER = 6
COEFFS = 152
DEEP = 160
STRENGTH = np.float32(0.04)
MESH = pl.DeviceIdType.MESH
BF = jnp.bfloat16
F32 = jnp.float32


def surface_coordinates():
    chosen = []
    for a in range(ORDER):
        for b in range(ORDER):
            for c in range(ORDER):
                if any(q in (0, ORDER - 1) for q in (a, b, c)):
                    chosen.append((a, b, c))
    lattice = np.array(chosen, np.int32).astype(np.float32)
    return lattice * np.float32(2.0 / (ORDER - 1)) - np.float32(1.0)


def translation_table():
    u = surface_coordinates()
    near = np.float32(0.525)
    squares = []
    for axis in range(3):
        target = near * u[:, axis]
        per = []
        for o in range(-3, 4):
            source = near * u[:, axis] + np.float32(o)
            per.append((target[None, :] - source[:, None]) ** 2)
        squares.append(np.stack(per))
    table = np.zeros((7, 7, 7, DEEP, COEFFS), ml_dtypes.bfloat16)
    for z in range(7):
        for y in range(7):
            for x in range(7):
                if max(abs(z - 3), abs(y - 3), abs(x - 3)) >= 2:
                    total = squares[0][z] + squares[1][y] + squares[2][x]
                    table[z, y, x, :COEFFS] = (STRENGTH / np.sqrt(total)).astype(ml_dtypes.bfloat16)
    return table


def transfer_table():
    u = surface_coordinates()
    table = np.zeros((8, DEEP, COEFFS), ml_dtypes.bfloat16)
    for k in range(8):
        bits = (k >> 2 & 1, k >> 1 & 1, k & 1)
        total = np.zeros((COEFFS, COEFFS), np.float32)
        for axis in range(3):
            child = np.float32(bits[axis]) - np.float32(0.5) + np.float32(0.525) * u[:, axis]
            parent = np.float32(2.95) * u[:, axis]
            total = total + (child[None, :] - parent[:, None]) ** 2
        table[k, :COEFFS] = (STRENGTH / np.sqrt(total)).astype(ml_dtypes.bfloat16)
    return table


def fine_selection():
    sel = np.zeros((6, 6, 4, 4, 8, 8), np.float32)
    for j in range(6):
        for m in range(6):
            for y in range(4):
                for x in range(4):
                    yy, xx = 2 * y + j - 2, 2 * x + m - 2
                    if 0 <= yy < 8 and 0 <= xx < 8:
                        sel[j, m, y, x, yy, xx] = 1
    return sel.reshape(576, 64)


def coarse_selection():
    sel = np.zeros((6, 6, 6, 4, 2, 2, 12, 4, 4), np.float32)
    for i in range(6):
        for j in range(6):
            for m in range(6):
                for z in range(4):
                    for y in range(2):
                        for x in range(2):
                            yy, xx = 2 * y + j - 2, 2 * x + m - 2
                            if 0 <= yy < 4 and 0 <= xx < 4:
                                sel[i, j, m, z, y, x, 2 * z + i, yy, xx] = 1
    return sel.reshape(6, 576, 192)


def parent_order():
    order = np.zeros((8, 4, 4, 2, 2, 2, 4, 2, 2), np.float32)
    for z in range(8):
        for y in range(4):
            for x in range(4):
                order[z, y, x, z % 2, y % 2, x % 2, z // 2, y // 2, x // 2] = 1
    return order.reshape(128, 128)


def kernel(
    leaves, fm, fp, cm, cp, cpx, inc, c2d, sel, selc, order, w_hbm, l_hbm, out,
    ext_f, ext_c, e_f, e_c, w_v, l_v, acc, inc_x, gath, w_sem, l_sem, hs, hr, gs, gr,
):
    leaf, rep = lax.axis_index("leaf"), lax.axis_index("rep")
    bz, by = rep // 2, rep % 2
    has_low, has_high = leaf > 0, leaf < leaves - 1
    barrier = pltpu.get_barrier_semaphore()

    def greet(where):
        pl.semaphore_signal(barrier, inc=1, device_id=where, device_id_type=MESH)

    @pl.when(has_low)
    def _():
        greet({"leaf": leaf - 1})

    @pl.when(has_high)
    def _():
        greet({"leaf": leaf + 1})

    for k in range(1, 4):
        greet({"rep": (rep + k) % 4})

    def weights(c):
        return pltpu.make_async_copy(
            w_hbm.at[c // 6 + 1 - bz, c % 6 + 1 - by], w_v.at[c], w_sem.at[c]
        )

    own_l = pltpu.make_async_copy(l_hbm.at[pl.ds(2 * rep, 2)], l_v, l_sem)

    def begin(c, carry):
        weights(c).start()
        return carry

    lax.fori_loop(0, 36, begin, 0)
    own_l.start()

    def eye(size):
        return (
            lax.broadcasted_iota(jnp.int32, (size, size), 0)
            == lax.broadcasted_iota(jnp.int32, (size, size), 1)
        ).astype(F32)

    eye_f, eye_c = eye(64), eye(16)
    for z in range(16):
        layer = fm[z].astype(F32).reshape(64, COEFFS).astype(BF)
        keep = (eye_f * fp[z].astype(F32)).astype(BF)
        ext_f[z + 2] = jnp.dot(keep, layer, preferred_element_type=F32).astype(BF)
    for z in range(8):
        keep = (eye_c * cp[z].astype(F32)).astype(BF)
        ext_c[z + 2] = jnp.dot(keep, cm[z], preferred_element_type=F32).astype(BF)

    @pl.when(jnp.logical_not(has_low))
    def _():
        ext_f[0:2] = jnp.zeros((2, 64, COEFFS), BF)
        ext_c[0:2] = jnp.zeros((2, 16, COEFFS), BF)

    @pl.when(jnp.logical_not(has_high))
    def _():
        ext_f[18:20] = jnp.zeros((2, 64, COEFFS), BF)
        ext_c[10:12] = jnp.zeros((2, 16, COEFFS), BF)

    pl.semaphore_wait(barrier, 3 + has_low.astype(jnp.int32) + has_high.astype(jnp.int32))

    def halo(ref, source, target, slot, step):
        return pltpu.make_async_remote_copy(
            src_ref=ref.at[pl.ds(source, 2)],
            dst_ref=ref.at[pl.ds(target, 2)],
            send_sem=hs.at[slot],
            recv_sem=hr.at[slot],
            device_id={"leaf": leaf + step},
            device_id_type=MESH,
        )

    def down():
        return halo(ext_f, 2, 18, 0, -1), halo(ext_c, 2, 10, 1, -1)

    def up():
        return halo(ext_f, 16, 0, 2, 1), halo(ext_c, 8, 0, 3, 1)

    @pl.when(has_low)
    def _():
        for copy in down():
            copy.start()

    @pl.when(has_high)
    def _():
        for copy in up():
            copy.start()

    def widen(z, carry):
        rows = jnp.dot(sel[...], ext_f[z], preferred_element_type=F32).astype(BF)
        e_f[:, z % 2, pl.ds(pl.multiple_of(z // 2 * 16, 16), 16), :] = rows.reshape(36, 16, COEFFS)
        return carry

    lax.fori_loop(2, 18, widen, 0)
    acc[...] = jnp.zeros_like(acc)
    inc_x[...] = jnp.zeros_like(inc_x)
    inc_x[32:160] = inc[...]

    @pl.when(has_low)
    def _():
        for copy in up():
            copy.wait_recv()

    @pl.when(has_high)
    def _():
        for copy in down():
            copy.wait_recv()

    for z in (0, 1, 18, 19):
        widen(z, 0)

    coarse = ext_c[...].reshape(192, COEFFS)

    def widen_coarse(i, carry):
        rows = jnp.dot(selc[i], coarse, preferred_element_type=F32).astype(BF)
        e_c[i] = rows.reshape(36, 16, COEFFS)
        return carry

    lax.fori_loop(0, 6, widen_coarse, 0)

    def step(c, carry):
        i, j = c // 6, c % 6
        weights(c).wait()
        first = pl.multiple_of(i // 2 * 16, 16)

        def window(m):
            return jnp.concatenate(
                [e_f[j * 6 + m, i % 2, pl.ds(first, 128), :], e_c[i, j * 6 + m]], axis=0
            )

        windows = [window(m) for m in range(6)]

        def times(rows, n):
            return jnp.dot(rows, w_v[c, n, :COEFFS], preferred_element_type=F32)

        total = jnp.concatenate([times(windows[5], 6), times(windows[0], 0)], axis=0)
        for n in range(1, 6):
            total += times(jnp.concatenate([windows[n - 1], windows[n]], axis=0), n)
        acc[...] += total
        return carry

    lax.fori_loop(0, 36, step, 0)

    base = pl.multiple_of(((by + 2) * 6 + 2) * 16, 16)
    own = selc[bz + 2, pl.ds(base, 32), :].astype(F32)
    arrived = jnp.dot(own, inc_x[...], precision=lax.Precision.HIGHEST, preferred_element_type=F32)
    present = jnp.sum(own * cpx[...].astype(F32), axis=1, keepdims=True)
    check = 0.5 * jnp.concatenate([acc[128:144], acc[272:288]], axis=0) + arrived
    dense = jnp.dot(check, c2d[...], precision=lax.Precision.HIGHEST, preferred_element_type=F32)
    gath[rep] = (2.0 * dense * present).astype(BF)

    def share(k):
        return pltpu.make_async_remote_copy(
            src_ref=gath.at[rep],
            dst_ref=gath.at[rep],
            send_sem=gs.at[k - 1],
            recv_sem=gr.at[k - 1],
            device_id={"rep": (rep + k) % 4},
            device_id_type=MESH,
        )

    def receive(k):
        return pltpu.make_async_remote_copy(
            src_ref=gath.at[rep],
            dst_ref=gath.at[(rep + 4 - k) % 4],
            send_sem=gs.at[k - 1],
            recv_sem=gr.at[k - 1],
            device_id={"rep": (rep + k) % 4},
            device_id_type=MESH,
        )

    for k in range(1, 4):
        share(k).start()
    own_l.wait()
    for k in range(1, 4):
        receive(k).wait_recv()
    parents = jnp.dot(
        order[...], gath[...].reshape(128, COEFFS), preferred_element_type=F32
    ).astype(BF)
    own_f = sel[pl.ds(base, 32), :].astype(F32)
    for bx in range(2):
        down_part = jnp.dot(parents, l_v[bx, :COEFFS], preferred_element_type=F32)
        fine_check = acc[bx * 144:bx * 144 + 128] + down_part
        dense = jnp.dot(
            fine_check, c2d[...], precision=lax.Precision.HIGHEST, preferred_element_type=F32
        )
        for z in range(8):
            there = jnp.sum(
                own_f[bx * 16:bx * 16 + 16] * fp[2 * z + bz].astype(F32), axis=1, keepdims=True
            )
            out[bx, z * 16:z * 16 + 16] = dense[z * 16:z * 16 + 16] * there

    for k in range(1, 4):
        share(k).wait_send()

    @pl.when(has_low)
    def _():
        for copy in down():
            copy.wait_send()

    @pl.when(has_high)
    def _():
        for copy in up():
            copy.wait_send()


def shards(leaves, tables, fm, fp, cm, cp, inc, c2d):
    w, l, sel, selc, order = tables
    cp_row = jnp.pad(cp.reshape(1, 128), ((0, 0), (32, 32)))
    vmem = pl.BlockSpec(memory_space=pltpu.VMEM)
    hbm = pl.BlockSpec(memory_space=pl.ANY)
    dma = pltpu.SemaphoreType.DMA
    out = pl.pallas_call(
        functools.partial(kernel, leaves),
        out_shape=jax.ShapeDtypeStruct((2, 128, COEFFS), F32),
        in_specs=[vmem] * 10 + [hbm] * 2,
        out_specs=vmem,
        scratch_shapes=[
            pltpu.VMEM((20, 64, COEFFS), BF),
            pltpu.VMEM((12, 16, COEFFS), BF),
            pltpu.VMEM((36, 2, 160, COEFFS), BF),
            pltpu.VMEM((6, 36, 16, COEFFS), BF),
            pltpu.VMEM((36, 7, DEEP, COEFFS), BF),
            pltpu.VMEM((2, DEEP, COEFFS), BF),
            pltpu.VMEM((288, COEFFS), F32),
            pltpu.VMEM((192, COEFFS), F32),
            pltpu.VMEM((4, 32, COEFFS), BF),
            dma((36,)),
            dma,
            dma((4,)),
            dma((4,)),
            dma((3,)),
            dma((3,)),
        ],
        compiler_params=pltpu.CompilerParams(
            collective_id=0, has_side_effects=True, vmem_limit_bytes=52 * 2**20
        ),
    )(
        fm,
        fp.reshape(16, 1, 64),
        cm.reshape(8, 16, COEFFS),
        cp.reshape(8, 1, 16),
        cp_row,
        inc.reshape(128, COEFFS),
        c2d,
        sel,
        selc,
        order,
        w,
        l,
    )
    return out.reshape(2, 8, 4, 4, COEFFS)


def solution(mesh):
    leaves = mesh.shape["leaf"]
    tables = (
        translation_table(),
        transfer_table(),
        fine_selection().astype(ml_dtypes.bfloat16),
        coarse_selection().astype(ml_dtypes.bfloat16),
        parent_order().astype(ml_dtypes.bfloat16),
    )
    in_specs = (
        P("leaf", None, None, None),
        P("leaf", None, None),
        P("leaf", None, None, None),
        P("leaf", None, None),
        P("leaf", None, None, None),
        P(),
    )

    def body(*args):
        return shards(leaves, tuple(jnp.asarray(t) for t in tables), *args)

    out_specs = P("rep", "leaf", None, None, None)
    return jax.shard_map(body, mesh=mesh, in_specs=in_specs, out_specs=out_specs, check_vma=False)
```

```python
import functools

import jax
import jax.numpy as jnp
import ml_dtypes
import numpy as np
from jax import lax
from jax.experimental import pallas as pl
from jax.experimental.pallas import tpu as pltpu
from jax.sharding import PartitionSpec as P

ORDER = 6
COEFFS = 152
DEEP = 160
STRENGTH = np.float32(0.04)
MESH = pl.DeviceIdType.MESH
BF = jnp.bfloat16
F32 = jnp.float32


def surface_coordinates():
    chosen = []
    for a in range(ORDER):
        for b in range(ORDER):
            for c in range(ORDER):
                if any(q in (0, ORDER - 1) for q in (a, b, c)):
                    chosen.append((a, b, c))
    lattice = np.array(chosen, np.int32).astype(np.float32)
    return lattice * np.float32(2.0 / (ORDER - 1)) - np.float32(1.0)


def translation_table():
    u = surface_coordinates()
    near = np.float32(0.525)
    squares = []
    for axis in range(3):
        target = near * u[:, axis]
        per = []
        for o in range(-3, 4):
            source = near * u[:, axis] + np.float32(o)
            per.append((target[None, :] - source[:, None]) ** 2)
        squares.append(np.stack(per))
    table = np.zeros((7, 7, 7, DEEP, COEFFS), ml_dtypes.bfloat16)
    for z in range(7):
        for y in range(7):
            for x in range(7):
                if max(abs(z - 3), abs(y - 3), abs(x - 3)) >= 2:
                    total = squares[0][z] + squares[1][y] + squares[2][x]
                    table[z, y, (x + 2) % 7, :COEFFS] = (STRENGTH / np.sqrt(total)).astype(ml_dtypes.bfloat16)
    return table


def transfer_table():
    u = surface_coordinates()
    table = np.zeros((8, DEEP, COEFFS), ml_dtypes.bfloat16)
    for k in range(8):
        bits = (k >> 2 & 1, k >> 1 & 1, k & 1)
        total = np.zeros((COEFFS, COEFFS), np.float32)
        for axis in range(3):
            child = np.float32(bits[axis]) - np.float32(0.5) + np.float32(0.525) * u[:, axis]
            parent = np.float32(2.95) * u[:, axis]
            total = total + (child[None, :] - parent[:, None]) ** 2
        table[k, :COEFFS] = (STRENGTH / np.sqrt(total)).astype(ml_dtypes.bfloat16)
    return table


def fine_selection():
    sel = np.zeros((6, 6, 4, 4, 8, 8), np.float32)
    for j in range(6):
        for m in range(6):
            for y in range(4):
                for x in range(4):
                    yy, xx = 2 * y + j - 2, 2 * x + m - 2
                    if 0 <= yy < 8 and 0 <= xx < 8:
                        sel[j, m, y, x, yy, xx] = 1
    return sel.reshape(576, 64)


def coarse_selection():
    sel = np.zeros((6, 6, 6, 4, 2, 2, 12, 4, 4), np.float32)
    for i in range(6):
        for j in range(6):
            for m in range(6):
                for z in range(4):
                    for y in range(2):
                        for x in range(2):
                            yy, xx = 2 * y + j - 2, 2 * x + m - 2
                            if 0 <= yy < 4 and 0 <= xx < 4:
                                sel[i, j, m, z, y, x, 2 * z + i, yy, xx] = 1
    return sel.reshape(6, 576, 192)


def parent_order():
    order = np.zeros((8, 4, 4, 2, 2, 2, 4, 2, 2), np.float32)
    for z in range(8):
        for y in range(4):
            for x in range(4):
                order[z, y, x, z % 2, y % 2, x % 2, z // 2, y // 2, x // 2] = 1
    return order.reshape(128, 128)


def kernel(
    leaves, fm_h, fp_h, cm_h, cp_h, inc_h, c2d_h, sel_h, selc_h, order_h, back_h, w_hbm, l_hbm, out,
    fm, fp, cm, cp, inc, c2d, sel, selc, order, back,
    ext_f, ext_c, e_f, e_c, w_v, l_v, acc, acc_c, mask_c, nat_c, nat_m, nat_i, gath,
    in_sem, w_sem, l_sem, hs, hr, gs, gr,
):
    leaf, rep = lax.axis_index("leaf"), lax.axis_index("rep")
    bz, by = rep // 2, rep % 2
    has_low, has_high = leaf > 0, leaf < leaves - 1
    barrier = pltpu.get_barrier_semaphore()

    def greet(where):
        pl.semaphore_signal(barrier, inc=1, device_id=where, device_id_type=MESH)

    @pl.when(has_low)
    def _():
        greet({"leaf": leaf - 1})

    @pl.when(has_high)
    def _():
        greet({"leaf": leaf + 1})

    for k in range(1, 4):
        greet({"rep": (rep + k) % 4})

    inputs = [
        pltpu.make_async_copy(source, target, in_sem.at[k])
        for k, (source, target) in enumerate(
            (
                (fp_h, fp), (fm_h, fm), (cp_h, cp), (cm_h, cm), (sel_h, sel), (selc_h, selc),
                (inc_h, inc), (c2d_h, c2d), (order_h, order), (back_h, back),
            )
        )
    ]
    for copy in inputs:
        copy.start()

    def place(a, b):
        return (a + 1 + bz) % 6, (b + 1 + by) % 6

    def weights(a, b, near):
        i, j = place(a, b)
        count = 4 if near else 7
        c = a * 6 + b
        return pltpu.make_async_copy(
            w_hbm.at[i + 1 - bz, j + 1 - by, pl.ds(0, count)],
            w_v.at[c, pl.ds(0, count)],
            w_sem.at[c],
        )

    own_l = pltpu.make_async_copy(l_hbm.at[pl.ds(2 * rep, 2)], l_v, l_sem)
    for a in range(6):
        for b in range(6):
            weights(a, b, a < 3 and b < 3).start()
    own_l.start()

    acc[...] = jnp.zeros_like(acc)
    acc_c[...] = jnp.zeros_like(acc_c)
    inputs[0].wait()
    mask_f = fp[...].astype(F32).reshape(64, 16)
    inputs[1].wait()
    for z in (0, 1, 14, 15) + tuple(range(2, 14)):
        layer = fm[z].astype(F32).reshape(64, COEFFS)
        ext_f[z + 2] = (layer * mask_f[:, z:z + 1]).astype(BF)
    inputs[2].wait()
    inputs[3].wait()
    for y in range(4):
        mask_c[4 * y:4 * y + 4] = cp[y].astype(F32)
    for z in range(8):
        for y in range(4):
            nat_c[16 * z + 4 * y:16 * z + 4 * y + 4] = cm[z, y].astype(F32)
    for z in range(8):
        keep = jnp.broadcast_to(mask_c[:, z:z + 1], (16, COEFFS))
        nat_m[16 * z:16 * z + 16] = keep.astype(BF)
        ext_c[z + 2] = (nat_c[16 * z:16 * z + 16] * keep).astype(BF)

    @pl.when(jnp.logical_not(has_low))
    def _():
        ext_f[0:2] = jnp.zeros((2, 64, COEFFS), BF)
        ext_c[0:2] = jnp.zeros((2, 16, COEFFS), BF)

    @pl.when(jnp.logical_not(has_high))
    def _():
        ext_f[18:20] = jnp.zeros((2, 64, COEFFS), BF)
        ext_c[10:12] = jnp.zeros((2, 16, COEFFS), BF)

    pl.semaphore_wait(barrier, 3 + has_low.astype(jnp.int32) + has_high.astype(jnp.int32))

    def halo(ref, source, target, slot, step):
        return pltpu.make_async_remote_copy(
            src_ref=ref.at[pl.ds(source, 2)],
            dst_ref=ref.at[pl.ds(target, 2)],
            send_sem=hs.at[slot],
            recv_sem=hr.at[slot],
            device_id={"leaf": leaf + step},
            device_id_type=MESH,
        )

    def down():
        return halo(ext_f, 2, 18, 0, -1), halo(ext_c, 2, 10, 1, -1)

    def up():
        return halo(ext_f, 16, 0, 2, 1), halo(ext_c, 8, 0, 3, 1)

    @pl.when(has_low)
    def _():
        for copy in down():
            copy.start()

    @pl.when(has_high)
    def _():
        for copy in up():
            copy.start()

    inputs[4].wait()

    def widen(z):
        rows = jnp.dot(sel[...], ext_f[z], preferred_element_type=F32).astype(BF)
        first = z // 2 * 16
        if not isinstance(z, int):
            first = pl.multiple_of(first, 16)
        e_f[:, z % 2, pl.ds(first, 16), :] = rows.reshape(36, 16, COEFFS)

    def widen_four(g, carry):
        for q in range(4):
            widen(2 + 4 * g + q)
        return carry

    lax.fori_loop(0, 4, widen_four, 0)
    for k in range(5, 10):
        inputs[k].wait()
    for z in range(8):
        for y in range(4):
            nat_i[16 * z + 4 * y:16 * z + 4 * y + 4] = inc[z, y]

    @pl.when(has_low)
    def _():
        for copy in up():
            copy.wait_recv()

    @pl.when(has_high)
    def _():
        for copy in down():
            copy.wait_recv()

    for z in (0, 1, 18, 19):
        widen(z)

    coarse = ext_c[...].reshape(192, COEFFS)

    def widen_coarse(g, carry):
        for q in range(2):
            i = 2 * g + q
            rows = jnp.dot(selc[i], coarse, preferred_element_type=F32).astype(BF)
            e_c[i] = rows.reshape(36, 16, COEFFS)
        return carry

    lax.fori_loop(0, 3, widen_coarse, 0)

    def visit(a, b, near, bx):
        i, j = place(a, b)
        c = a * 6 + b
        first = pl.multiple_of(i // 2 * 16, 16)
        if bx == 0:
            weights(a, b, near).wait()

        def fine(m):
            return e_f[j * 6 + m, i % 2, pl.ds(first, 128), :]

        def small(m):
            return e_c[i, j * 6 + m]

        def times(rows, n):
            return jnp.dot(rows, w_v[c, (n + 2) % 7, :COEFFS], preferred_element_type=F32)

        middle = (1, 5) if near else (1, 2, 3, 4, 5)
        if bx == 1:
            total = times(fine(0), 0)
            for n in middle:
                total += times(fine(n), n)
            acc[1] += total
            return
        total = None
        for n in middle:
            term = times(jnp.concatenate([fine(n - 1), small(n - 1), small(n)], axis=0), n)
            total = term if total is None else total + term
        last = times(jnp.concatenate([fine(5), small(5)], axis=0), 6)
        acc[0] += total[:128] + last[:128]
        acc_c[0] += total[128:144] + last[128:]
        acc_c[1] += total[144:] + times(small(0), 0)

    def sweep(bx):
        def some(a, carry):
            for b in range(6):
                visit(a, b, b < 3, bx)
            return carry

        def rest(a, carry):
            for b in range(6):
                visit(a, b, False, bx)
            return carry

        lax.fori_loop(0, 3, some, 0)
        lax.fori_loop(3, 6, rest, 0)

    sweep(0)

    own = back[pl.ds(pl.multiple_of(rep * 32, 32), 32), :]
    arrived = jnp.dot(
        own.astype(F32), nat_i[...], precision=lax.Precision.HIGHEST, preferred_element_type=F32
    )
    present = jnp.dot(own, nat_m[...], preferred_element_type=F32)
    check = 0.5 * jnp.concatenate([acc_c[0], acc_c[1]], axis=0) + arrived
    dense = jnp.dot(check, c2d[...], precision=lax.Precision.HIGHEST, preferred_element_type=F32)
    gath[rep] = (2.0 * dense * present).astype(BF)

    def share(k):
        return pltpu.make_async_remote_copy(
            src_ref=gath.at[rep],
            dst_ref=gath.at[rep],
            send_sem=gs.at[k - 1],
            recv_sem=gr.at[k - 1],
            device_id={"rep": (rep + k) % 4},
            device_id_type=MESH,
        )

    def receive(k):
        return pltpu.make_async_remote_copy(
            src_ref=gath.at[rep],
            dst_ref=gath.at[(rep + 4 - k) % 4],
            send_sem=gs.at[k - 1],
            recv_sem=gr.at[k - 1],
            device_id={"rep": (rep + k) % 4},
            device_id_type=MESH,
        )

    for k in range(1, 4):
        share(k).start()

    sweep(1)

    own_l.wait()
    for k in range(1, 4):
        receive(k).wait_recv()
    parents = jnp.dot(
        order[...], gath[...].reshape(128, COEFFS), preferred_element_type=F32
    ).astype(BF)
    base = pl.multiple_of(((by + 2) * 6 + 2) * 16, 16)
    there = jnp.dot(sel[pl.ds(base, 32), :], mask_f.astype(BF), preferred_element_type=F32)
    for bx in range(2):
        down_part = jnp.dot(parents, l_v[bx, :COEFFS], preferred_element_type=F32)
        dense = jnp.dot(
            acc[bx] + down_part, c2d[...], precision=lax.Precision.HIGHEST, preferred_element_type=F32
        )
        for z in range(8):
            rows = slice(bx * 16, bx * 16 + 16)
            kept = jnp.where(bz == 1, there[rows, 2 * z + 1:2 * z + 2], there[rows, 2 * z:2 * z + 1])
            layer = dense[z * 16:z * 16 + 16] * kept
            for y in range(4):
                out[bx, z, y] = layer[4 * y:4 * y + 4]

    for k in range(1, 4):
        share(k).wait_send()

    @pl.when(has_low)
    def _():
        for copy in down():
            copy.wait_send()

    @pl.when(has_high)
    def _():
        for copy in up():
            copy.wait_send()


def shards(leaves, tables, fm, fp, cm, cp, inc, c2d):
    w, l, sel, selc, order = tables
    operands = (
        fm, fp.transpose(1, 2, 0), cm, cp.transpose(1, 2, 0), inc, c2d,
        sel, selc, order, order.T, w, l,
    )
    vmem = pl.BlockSpec(memory_space=pltpu.VMEM)
    hbm = pl.BlockSpec(memory_space=pltpu.HBM)
    dma = pltpu.SemaphoreType.DMA
    operands = tuple(jnp.asarray(t) for t in operands)
    return pl.pallas_call(
        functools.partial(kernel, leaves),
        out_shape=jax.ShapeDtypeStruct((2, 8, 4, 4, COEFFS), F32),
        in_specs=[hbm] * 12,
        out_specs=vmem,
        scratch_shapes=[pltpu.VMEM(t.shape, t.dtype) for t in operands[:10]]
        + [
            pltpu.VMEM((20, 64, COEFFS), BF),
            pltpu.VMEM((12, 16, COEFFS), BF),
            pltpu.VMEM((36, 2, 160, COEFFS), BF),
            pltpu.VMEM((6, 36, 16, COEFFS), BF),
            pltpu.VMEM((36, 7, DEEP, COEFFS), BF),
            pltpu.VMEM((2, DEEP, COEFFS), BF),
            pltpu.VMEM((2, 128, COEFFS), F32),
            pltpu.VMEM((2, 16, COEFFS), F32),
            pltpu.VMEM((16, 8), F32),
            pltpu.VMEM((128, COEFFS), F32),
            pltpu.VMEM((128, COEFFS), BF),
            pltpu.VMEM((128, COEFFS), F32),
            pltpu.VMEM((4, 32, COEFFS), BF),
            dma((10,)),
            dma((36,)),
            dma,
            dma((4,)),
            dma((4,)),
            dma((3,)),
            dma((3,)),
        ],
        compiler_params=pltpu.CompilerParams(
            collective_id=0, has_side_effects=True, vmem_limit_bytes=52 * 2**20
        ),
    )(*operands)


def solution(mesh):
    leaves = mesh.shape["leaf"]
    tables = (
        translation_table(),
        transfer_table(),
        fine_selection().astype(ml_dtypes.bfloat16),
        coarse_selection().astype(ml_dtypes.bfloat16),
        parent_order().astype(ml_dtypes.bfloat16),
    )
    in_specs = (
        P("leaf", None, None, None),
        P("leaf", None, None),
        P("leaf", None, None, None),
        P("leaf", None, None),
        P("leaf", None, None, None),
        P(),
    )

    def body(*args):
        return shards(leaves, tables, *args)

    out_specs = P("rep", "leaf", None, None, None)
    return jax.shard_map(body, mesh=mesh, in_specs=in_specs, out_specs=out_specs, check_vma=False)
```

```python
import functools

import jax
import jax.numpy as jnp
import ml_dtypes
import numpy as np
from jax import lax
from jax.experimental import pallas as pl
from jax.experimental.pallas import tpu as pltpu
from jax.sharding import PartitionSpec as P

ORDER = 6
COEFFS = 152
DEEP = 160
STRENGTH = np.float32(0.04)
MESH = pl.DeviceIdType.MESH
BF = jnp.bfloat16
F32 = jnp.float32


def surface_coordinates():
    chosen = []
    for a in range(ORDER):
        for b in range(ORDER):
            for c in range(ORDER):
                if any(q in (0, ORDER - 1) for q in (a, b, c)):
                    chosen.append((a, b, c))
    lattice = np.array(chosen, np.int32).astype(np.float32)
    return lattice * np.float32(2.0 / (ORDER - 1)) - np.float32(1.0)


def translation_table():
    u = surface_coordinates()
    near = np.float32(0.525)
    squares = []
    for axis in range(3):
        target = near * u[:, axis]
        per = []
        for o in range(-3, 4):
            source = near * u[:, axis] + np.float32(o)
            per.append((target[None, :] - source[:, None]) ** 2)
        squares.append(np.stack(per))
    table = np.zeros((7, 7, 7, DEEP, COEFFS), ml_dtypes.bfloat16)
    for z in range(7):
        for y in range(7):
            for x in range(7):
                if max(abs(z - 3), abs(y - 3), abs(x - 3)) >= 2:
                    total = squares[0][z] + squares[1][y] + squares[2][x]
                    table[z, y, (x + 2) % 7, :COEFFS] = (STRENGTH / np.sqrt(total)).astype(ml_dtypes.bfloat16)
    return table


def transfer_table():
    u = surface_coordinates()
    table = np.zeros((8, DEEP, COEFFS), ml_dtypes.bfloat16)
    for k in range(8):
        bits = (k >> 2 & 1, k >> 1 & 1, k & 1)
        total = np.zeros((COEFFS, COEFFS), np.float32)
        for axis in range(3):
            child = np.float32(bits[axis]) - np.float32(0.5) + np.float32(0.525) * u[:, axis]
            parent = np.float32(2.95) * u[:, axis]
            total = total + (child[None, :] - parent[:, None]) ** 2
        table[k, :COEFFS] = (STRENGTH / np.sqrt(total)).astype(ml_dtypes.bfloat16)
    return table


def fine_selection():
    sel = np.zeros((6, 6, 4, 4, 8, 8), np.float32)
    for j in range(6):
        for m in range(6):
            for y in range(4):
                for x in range(4):
                    yy, xx = 2 * y + j - 2, 2 * x + m - 2
                    if 0 <= yy < 8 and 0 <= xx < 8:
                        sel[j, m, y, x, yy, xx] = 1
    return sel.reshape(576, 64)


def coarse_selection():
    sel = np.zeros((6, 6, 6, 4, 2, 2, 12, 4, 4), np.float32)
    for i in range(6):
        for j in range(6):
            for m in range(6):
                for z in range(4):
                    for y in range(2):
                        for x in range(2):
                            yy, xx = 2 * y + j - 2, 2 * x + m - 2
                            if 0 <= yy < 4 and 0 <= xx < 4:
                                sel[i, j, m, z, y, x, 2 * z + i, yy, xx] = 1
    return sel.reshape(6, 576, 192)


def parent_order():
    order = np.zeros((8, 4, 4, 2, 2, 2, 4, 2, 2), np.float32)
    for z in range(8):
        for y in range(4):
            for x in range(4):
                order[z, y, x, z % 2, y % 2, x % 2, z // 2, y // 2, x // 2] = 1
    return order.reshape(128, 128)


def kernel(
    leaves, fm_h, fp_h, cm_h, cp_h, inc_h, c2d_h, sel_h, selc_h, order_h, back_h, w_hbm, l_hbm, out,
    fm, fp, cm, cp, inc, c2d, sel, selc, order, back,
    ext_f, ext_c, e_f, e_c, w_v, l_v, acc, acc_c, mask_c, nat_c, nat_m, nat_i, gath,
    in_sem, w_sem, l_sem, hs, hr, gs, gr,
):
    leaf, rep = lax.axis_index("leaf"), lax.axis_index("rep")
    bz, by = rep // 2, rep % 2
    has_low, has_high = leaf > 0, leaf < leaves - 1
    barrier = pltpu.get_barrier_semaphore()

    def greet(where):
        pl.semaphore_signal(barrier, inc=1, device_id=where, device_id_type=MESH)

    @pl.when(has_low)
    def _():
        greet({"leaf": leaf - 1})

    @pl.when(has_high)
    def _():
        greet({"leaf": leaf + 1})

    for k in range(1, 4):
        greet({"rep": (rep + k) % 4})

    inputs = [
        pltpu.make_async_copy(source, target, in_sem.at[k])
        for k, (source, target) in enumerate(
            (
                (fp_h, fp), (fm_h, fm), (cp_h, cp), (cm_h, cm), (sel_h, sel), (selc_h, selc),
                (inc_h, inc), (c2d_h, c2d), (order_h, order), (back_h, back),
            )
        )
    ]
    for copy in inputs:
        copy.start()

    def place(a, b):
        return (a + 1 + bz) % 6, (b + 1 + by) % 6

    def weights(a, b, near):
        i, j = place(a, b)
        count = 4 if near else 7
        c = a * 6 + b
        return pltpu.make_async_copy(
            w_hbm.at[i + 1 - bz, j + 1 - by, pl.ds(0, count)],
            w_v.at[c, pl.ds(0, count)],
            w_sem.at[c],
        )

    own_l = pltpu.make_async_copy(l_hbm.at[pl.ds(2 * rep, 2)], l_v, l_sem)
    for a in range(6):
        for b in range(6):
            weights(a, b, a < 3 and b < 3).start()
    own_l.start()

    acc[...] = jnp.zeros_like(acc)
    acc_c[...] = jnp.zeros_like(acc_c)
    inputs[0].wait()
    mask_f = fp[...].astype(F32).reshape(64, 16)
    inputs[1].wait()
    for z in (0, 1, 14, 15) + tuple(range(2, 14)):
        layer = fm[z].astype(F32).reshape(64, COEFFS)
        ext_f[z + 2] = (layer * mask_f[:, z:z + 1]).astype(BF)
    inputs[2].wait()
    inputs[3].wait()
    for y in range(4):
        mask_c[4 * y:4 * y + 4] = cp[y].astype(F32)
    for z in range(8):
        for y in range(4):
            nat_c[16 * z + 4 * y:16 * z + 4 * y + 4] = cm[z, y].astype(F32)
    for z in range(8):
        keep = jnp.broadcast_to(mask_c[:, z:z + 1], (16, COEFFS))
        nat_m[16 * z:16 * z + 16] = keep.astype(BF)
        ext_c[z + 2] = (nat_c[16 * z:16 * z + 16] * keep).astype(BF)

    @pl.when(jnp.logical_not(has_low))
    def _():
        ext_f[0:2] = jnp.zeros((2, 64, COEFFS), BF)
        ext_c[0:2] = jnp.zeros((2, 16, COEFFS), BF)

    @pl.when(jnp.logical_not(has_high))
    def _():
        ext_f[18:20] = jnp.zeros((2, 64, COEFFS), BF)
        ext_c[10:12] = jnp.zeros((2, 16, COEFFS), BF)

    pl.semaphore_wait(barrier, 3 + has_low.astype(jnp.int32) + has_high.astype(jnp.int32))

    def halo(ref, source, target, slot, step):
        return pltpu.make_async_remote_copy(
            src_ref=ref.at[pl.ds(source, 2)],
            dst_ref=ref.at[pl.ds(target, 2)],
            send_sem=hs.at[slot],
            recv_sem=hr.at[slot],
            device_id={"leaf": leaf + step},
            device_id_type=MESH,
        )

    def down():
        return halo(ext_f, 2, 18, 0, -1), halo(ext_c, 2, 10, 1, -1)

    def up():
        return halo(ext_f, 16, 0, 2, 1), halo(ext_c, 8, 0, 3, 1)

    @pl.when(has_low)
    def _():
        for copy in down():
            copy.start()

    @pl.when(has_high)
    def _():
        for copy in up():
            copy.start()

    inputs[4].wait()

    def widen(z):
        rows = jnp.dot(sel[...], ext_f[z], preferred_element_type=F32).astype(BF)
        first = z // 2 * 16
        if not isinstance(z, int):
            first = pl.multiple_of(first, 16)
        e_f[:, z % 2, pl.ds(first, 16), :] = rows.reshape(36, 16, COEFFS)

    def widen_four(g, carry):
        for q in range(4):
            widen(2 + 4 * g + q)
        return carry

    lax.fori_loop(0, 4, widen_four, 0, unroll=4)
    for k in range(5, 10):
        inputs[k].wait()
    for z in range(8):
        for y in range(4):
            nat_i[16 * z + 4 * y:16 * z + 4 * y + 4] = inc[z, y]

    @pl.when(has_low)
    def _():
        for copy in up():
            copy.wait_recv()

    @pl.when(has_high)
    def _():
        for copy in down():
            copy.wait_recv()

    for z in (0, 1, 18, 19):
        widen(z)

    coarse = ext_c[...].reshape(192, COEFFS)

    def widen_coarse(g, carry):
        for q in range(2):
            i = 2 * g + q
            rows = jnp.dot(selc[i], coarse, preferred_element_type=F32).astype(BF)
            e_c[i] = rows.reshape(36, 16, COEFFS)
        return carry

    lax.fori_loop(0, 3, widen_coarse, 0, unroll=3)

    def visit(a, b, near, bx):
        i, j = place(a, b)
        c = a * 6 + b
        first = pl.multiple_of(i // 2 * 16, 16)

        def fine(m):
            return e_f[j * 6 + m, i % 2, pl.ds(first, 128), :]

        def small(m):
            return e_c[i, j * 6 + m]

        def times(rows, n):
            return jnp.dot(rows, w_v[c, (n + 2) % 7, :COEFFS], preferred_element_type=F32)

        middle = (1, 5) if near else (1, 2, 3, 4, 5)
        if bx == 1:
            total = times(fine(0), 0)
            for n in middle:
                total += times(fine(n), n)
            acc[1] += total
            return
        total = None
        for n in middle:
            term = times(jnp.concatenate([fine(n - 1), small(n - 1), small(n)], axis=0), n)
            total = term if total is None else total + term
        last = times(jnp.concatenate([fine(5), small(5)], axis=0), 6)
        acc[0] += total[:128] + last[:128]
        acc_c[0] += total[128:144] + last[128:]
        acc_c[1] += total[144:] + times(small(0), 0)

    def sweep(bx):
        def ready(a, close):
            if bx == 0:
                for b in range(6):
                    weights(a, b, close and b < 3).wait()

        def some(a, carry):
            ready(a, True)
            for b in range(6):
                visit(a, b, b < 3, bx)
            return carry

        def rest(a, carry):
            ready(a, False)
            for b in range(6):
                visit(a, b, False, bx)
            return carry

        lax.fori_loop(0, 3, some, 0, unroll=3)
        lax.fori_loop(3, 6, rest, 0, unroll=3)

    sweep(0)

    own = back[pl.ds(pl.multiple_of(rep * 32, 32), 32), :]
    arrived = jnp.dot(
        own.astype(F32), nat_i[...], precision=lax.Precision.HIGHEST, preferred_element_type=F32
    )
    present = jnp.dot(own, nat_m[...], preferred_element_type=F32)
    check = 0.5 * jnp.concatenate([acc_c[0], acc_c[1]], axis=0) + arrived
    dense = jnp.dot(check, c2d[...], precision=lax.Precision.HIGHEST, preferred_element_type=F32)
    gath[rep] = (2.0 * dense * present).astype(BF)

    def share(k):
        return pltpu.make_async_remote_copy(
            src_ref=gath.at[rep],
            dst_ref=gath.at[rep],
            send_sem=gs.at[k - 1],
            recv_sem=gr.at[k - 1],
            device_id={"rep": (rep + k) % 4},
            device_id_type=MESH,
        )

    def receive(k):
        return pltpu.make_async_remote_copy(
            src_ref=gath.at[rep],
            dst_ref=gath.at[(rep + 4 - k) % 4],
            send_sem=gs.at[k - 1],
            recv_sem=gr.at[k - 1],
            device_id={"rep": (rep + k) % 4},
            device_id_type=MESH,
        )

    for k in range(1, 4):
        share(k).start()

    sweep(1)

    own_l.wait()
    for k in range(1, 4):
        receive(k).wait_recv()
    parents = jnp.dot(
        order[...], gath[...].reshape(128, COEFFS), preferred_element_type=F32
    ).astype(BF)
    base = pl.multiple_of(((by + 2) * 6 + 2) * 16, 16)
    there = jnp.dot(sel[pl.ds(base, 32), :], mask_f.astype(BF), preferred_element_type=F32)
    for bx in range(2):
        down_part = jnp.dot(parents, l_v[bx, :COEFFS], preferred_element_type=F32)
        dense = jnp.dot(
            acc[bx] + down_part, c2d[...], precision=lax.Precision.HIGHEST, preferred_element_type=F32
        )
        for z in range(8):
            rows = slice(bx * 16, bx * 16 + 16)
            kept = jnp.where(bz == 1, there[rows, 2 * z + 1:2 * z + 2], there[rows, 2 * z:2 * z + 1])
            layer = dense[z * 16:z * 16 + 16] * kept
            for y in range(4):
                out[bx, z, y] = layer[4 * y:4 * y + 4]

    for k in range(1, 4):
        share(k).wait_send()

    @pl.when(has_low)
    def _():
        for copy in down():
            copy.wait_send()

    @pl.when(has_high)
    def _():
        for copy in up():
            copy.wait_send()


def shards(leaves, tables, fm, fp, cm, cp, inc, c2d):
    w, l, sel, selc, order = tables
    operands = (
        fm, fp.transpose(1, 2, 0), cm, cp.transpose(1, 2, 0), inc, c2d,
        sel, selc, order, order.T, w, l,
    )
    vmem = pl.BlockSpec(memory_space=pltpu.VMEM)
    hbm = pl.BlockSpec(memory_space=pltpu.HBM)
    dma = pltpu.SemaphoreType.DMA
    operands = tuple(jnp.asarray(t) for t in operands)
    return pl.pallas_call(
        functools.partial(kernel, leaves),
        out_shape=jax.ShapeDtypeStruct((2, 8, 4, 4, COEFFS), F32),
        in_specs=[hbm] * 12,
        out_specs=vmem,
        scratch_shapes=[pltpu.VMEM(t.shape, t.dtype) for t in operands[:10]]
        + [
            pltpu.VMEM((20, 64, COEFFS), BF),
            pltpu.VMEM((12, 16, COEFFS), BF),
            pltpu.VMEM((36, 2, 160, COEFFS), BF),
            pltpu.VMEM((6, 36, 16, COEFFS), BF),
            pltpu.VMEM((36, 7, DEEP, COEFFS), BF),
            pltpu.VMEM((2, DEEP, COEFFS), BF),
            pltpu.VMEM((2, 128, COEFFS), F32),
            pltpu.VMEM((2, 16, COEFFS), F32),
            pltpu.VMEM((16, 8), F32),
            pltpu.VMEM((128, COEFFS), F32),
            pltpu.VMEM((128, COEFFS), BF),
            pltpu.VMEM((128, COEFFS), F32),
            pltpu.VMEM((4, 32, COEFFS), BF),
            dma((10,)),
            dma((36,)),
            dma,
            dma((4,)),
            dma((4,)),
            dma((3,)),
            dma((3,)),
        ],
        compiler_params=pltpu.CompilerParams(
            collective_id=0, has_side_effects=True, vmem_limit_bytes=63 * 2**20
        ),
    )(*operands)


def solution(mesh):
    leaves = mesh.shape["leaf"]
    tables = (
        translation_table(),
        transfer_table(),
        fine_selection().astype(ml_dtypes.bfloat16),
        coarse_selection().astype(ml_dtypes.bfloat16),
        parent_order().astype(ml_dtypes.bfloat16),
    )
    in_specs = (
        P("leaf", None, None, None),
        P("leaf", None, None),
        P("leaf", None, None, None),
        P("leaf", None, None),
        P("leaf", None, None, None),
        P(),
    )

    def body(*args):
        return shards(leaves, tables, *args)

    out_specs = P("rep", "leaf", None, None, None)
    return jax.shard_map(body, mesh=mesh, in_specs=in_specs, out_specs=out_specs, check_vma=False)
```

```python
import functools

import jax
import jax.numpy as jnp
import ml_dtypes
import numpy as np
from jax import lax
from jax.experimental import pallas as pl
from jax.experimental.pallas import tpu as pltpu
from jax.sharding import PartitionSpec as P

ORDER = 6
COEFFS = 152
DEEP = 160
STRENGTH = np.float32(0.04)
MESH = pl.DeviceIdType.MESH
BF = jnp.bfloat16
F32 = jnp.float32


def surface_coordinates():
    chosen = []
    for a in range(ORDER):
        for b in range(ORDER):
            for c in range(ORDER):
                if any(q in (0, ORDER - 1) for q in (a, b, c)):
                    chosen.append((a, b, c))
    lattice = np.array(chosen, np.int32).astype(np.float32)
    return lattice * np.float32(2.0 / (ORDER - 1)) - np.float32(1.0)


def translation_table():
    u = surface_coordinates()
    near = np.float32(0.525)
    squares = []
    for axis in range(3):
        target = near * u[:, axis]
        per = []
        for o in range(-3, 4):
            source = near * u[:, axis] + np.float32(o)
            per.append((target[None, :] - source[:, None]) ** 2)
        squares.append(np.stack(per))
    table = np.zeros((7, 7, 7, DEEP, COEFFS), ml_dtypes.bfloat16)
    for z in range(7):
        for y in range(7):
            for x in range(7):
                if max(abs(z - 3), abs(y - 3), abs(x - 3)) >= 2:
                    total = squares[0][z] + squares[1][y] + squares[2][x]
                    table[z, y, (x + 2) % 7, :COEFFS] = (STRENGTH / np.sqrt(total)).astype(ml_dtypes.bfloat16)
    return table


def transfer_table():
    u = surface_coordinates()
    table = np.zeros((8, DEEP, COEFFS), ml_dtypes.bfloat16)
    for k in range(8):
        bits = (k >> 2 & 1, k >> 1 & 1, k & 1)
        total = np.zeros((COEFFS, COEFFS), np.float32)
        for axis in range(3):
            child = np.float32(bits[axis]) - np.float32(0.5) + np.float32(0.525) * u[:, axis]
            parent = np.float32(2.95) * u[:, axis]
            total = total + (child[None, :] - parent[:, None]) ** 2
        table[k, :COEFFS] = (STRENGTH / np.sqrt(total)).astype(ml_dtypes.bfloat16)
    return table


def fine_selection():
    sel = np.zeros((6, 6, 4, 4, 8, 8), np.float32)
    for j in range(6):
        for m in range(6):
            for y in range(4):
                for x in range(4):
                    yy, xx = 2 * y + j - 2, 2 * x + m - 2
                    if 0 <= yy < 8 and 0 <= xx < 8:
                        sel[j, m, y, x, yy, xx] = 1
    return sel.reshape(576, 64)


def coarse_selection():
    sel = np.zeros((6, 6, 6, 4, 2, 2, 12, 4, 4), np.float32)
    for i in range(6):
        for j in range(6):
            for m in range(6):
                for z in range(4):
                    for y in range(2):
                        for x in range(2):
                            yy, xx = 2 * y + j - 2, 2 * x + m - 2
                            if 0 <= yy < 4 and 0 <= xx < 4:
                                sel[i, j, m, z, y, x, 2 * z + i, yy, xx] = 1
    return sel.reshape(6, 576, 192)


def parent_order():
    order = np.zeros((8, 4, 4, 2, 2, 2, 4, 2, 2), np.float32)
    for z in range(8):
        for y in range(4):
            for x in range(4):
                order[z, y, x, z % 2, y % 2, x % 2, z // 2, y // 2, x // 2] = 1
    return order.reshape(128, 128)


def kernel(
    leaves, fm_h, fp_h, cm_h, cp_h, inc_h, c2d_h, sel_h, selc_h, order_h, back_h, w_hbm, l_hbm, out,
    fm, fp, cm, cp, inc, c2d, sel, selc, order, back,
    ext_f, ext_c, e_f, e_c, w_v, l_v, acc, acc_c, mask_c, nat_c, nat_m, nat_i, gath,
    in_sem, w_sem, l_sem, hs, hr, gs, gr,
):
    leaf, rep = lax.axis_index("leaf"), lax.axis_index("rep")
    bz, by = rep // 2, rep % 2
    has_low, has_high = leaf > 0, leaf < leaves - 1
    barrier = pltpu.get_barrier_semaphore()

    def greet(where):
        pl.semaphore_signal(barrier, inc=1, device_id=where, device_id_type=MESH)

    @pl.when(has_low)
    def _():
        greet({"leaf": leaf - 1})

    @pl.when(has_high)
    def _():
        greet({"leaf": leaf + 1})

    for k in range(1, 4):
        greet({"rep": (rep + k) % 4})

    inputs = [
        pltpu.make_async_copy(source, target, in_sem.at[k])
        for k, (source, target) in enumerate(
            (
                (fp_h, fp), (fm_h, fm), (cp_h, cp), (cm_h, cm), (sel_h, sel), (selc_h, selc),
                (inc_h, inc), (c2d_h, c2d), (order_h, order), (back_h, back),
            )
        )
    ]
    for copy in inputs:
        copy.start()

    def place(a, b):
        return (a + 1 + bz) % 6, (b + 1 + by) % 6

    def weights(a, b, near):
        i, j = place(a, b)
        count = 4 if near else 7
        c = a * 6 + b
        return pltpu.make_async_copy(
            w_hbm.at[i + 1 - bz, j + 1 - by, pl.ds(0, count)],
            w_v.at[c, pl.ds(0, count)],
            w_sem.at[c],
        )

    own_l = pltpu.make_async_copy(l_hbm.at[pl.ds(2 * rep, 2)], l_v, l_sem)
    for a in range(2):
        for b in range(6):
            weights(a, b, a < 3 and b < 3).start()

    acc[...] = jnp.zeros_like(acc)
    acc_c[...] = jnp.zeros_like(acc_c)
    inputs[0].wait()
    mask_f = fp[...].astype(F32).reshape(64, 16)
    inputs[1].wait()
    for z in (0, 1, 14, 15) + tuple(range(2, 14)):
        layer = fm[z].astype(F32).reshape(64, COEFFS)
        ext_f[z + 2] = (layer * mask_f[:, z:z + 1]).astype(BF)
    inputs[2].wait()
    inputs[3].wait()
    for y in range(4):
        mask_c[4 * y:4 * y + 4] = cp[y].astype(F32)
    for z in range(8):
        for y in range(4):
            nat_c[16 * z + 4 * y:16 * z + 4 * y + 4] = cm[z, y].astype(F32)
    for z in range(8):
        keep = jnp.broadcast_to(mask_c[:, z:z + 1], (16, COEFFS))
        nat_m[16 * z:16 * z + 16] = keep.astype(BF)
        ext_c[z + 2] = (nat_c[16 * z:16 * z + 16] * keep).astype(BF)

    @pl.when(jnp.logical_not(has_low))
    def _():
        ext_f[0:2] = jnp.zeros((2, 64, COEFFS), BF)
        ext_c[0:2] = jnp.zeros((2, 16, COEFFS), BF)

    @pl.when(jnp.logical_not(has_high))
    def _():
        ext_f[18:20] = jnp.zeros((2, 64, COEFFS), BF)
        ext_c[10:12] = jnp.zeros((2, 16, COEFFS), BF)

    pl.semaphore_wait(barrier, 3 + has_low.astype(jnp.int32) + has_high.astype(jnp.int32))

    def halo(ref, source, target, slot, step):
        return pltpu.make_async_remote_copy(
            src_ref=ref.at[pl.ds(source, 2)],
            dst_ref=ref.at[pl.ds(target, 2)],
            send_sem=hs.at[slot],
            recv_sem=hr.at[slot],
            device_id={"leaf": leaf + step},
            device_id_type=MESH,
        )

    def down():
        return halo(ext_f, 2, 18, 0, -1), halo(ext_c, 2, 10, 1, -1)

    def up():
        return halo(ext_f, 16, 0, 2, 1), halo(ext_c, 8, 0, 3, 1)

    @pl.when(has_low)
    def _():
        for copy in down():
            copy.start()

    @pl.when(has_high)
    def _():
        for copy in up():
            copy.start()

    for a in range(2, 6):
        for b in range(6):
            weights(a, b, a < 3 and b < 3).start()
    own_l.start()
    inputs[4].wait()

    def widen(z):
        rows = jnp.dot(sel[...], ext_f[z], preferred_element_type=F32).astype(BF)
        first = z // 2 * 16
        if not isinstance(z, int):
            first = pl.multiple_of(first, 16)
        e_f[:, z % 2, pl.ds(first, 16), :] = rows.reshape(36, 16, COEFFS)

    def widen_four(g, carry):
        for q in range(4):
            widen(2 + 4 * g + q)
        return carry

    lax.fori_loop(0, 4, widen_four, 0, unroll=4)
    for k in range(5, 10):
        inputs[k].wait()
    for z in range(8):
        for y in range(4):
            nat_i[16 * z + 4 * y:16 * z + 4 * y + 4] = inc[z, y]

    @pl.when(has_low)
    def _():
        for copy in up():
            copy.wait_recv()

    @pl.when(has_high)
    def _():
        for copy in down():
            copy.wait_recv()

    for z in (0, 1, 18, 19):
        widen(z)

    coarse = ext_c[...].reshape(192, COEFFS)

    def widen_coarse(g, carry):
        for q in range(2):
            i = 2 * g + q
            rows = jnp.dot(selc[i], coarse, preferred_element_type=F32).astype(BF)
            e_c[i] = rows.reshape(36, 16, COEFFS)
        return carry

    lax.fori_loop(0, 3, widen_coarse, 0, unroll=3)

    def visit(a, b, near, bx):
        i, j = place(a, b)
        c = a * 6 + b
        first = pl.multiple_of(i // 2 * 16, 16)

        def fine(m):
            return e_f[j * 6 + m, i % 2, pl.ds(first, 128), :]

        def small(m):
            return e_c[i, j * 6 + m]

        def times(rows, n):
            return jnp.dot(rows, w_v[c, (n + 2) % 7, :COEFFS], preferred_element_type=F32)

        middle = (1, 5) if near else (1, 2, 3, 4, 5)
        if bx == 1:
            total = times(fine(0), 0)
            for n in middle:
                total += times(fine(n), n)
            acc[1] += total
            return
        total = None
        for n in middle:
            term = times(jnp.concatenate([fine(n - 1), small(n - 1), small(n)], axis=0), n)
            total = term if total is None else total + term
        last = times(jnp.concatenate([fine(5), small(5)], axis=0), 6)
        acc[0] += total[:128] + last[:128]
        acc_c[0] += total[128:144] + last[128:]
        acc_c[1] += total[144:] + times(small(0), 0)

    def sweep(bx):
        def ready(a, close):
            if bx == 0:
                for b in range(6):
                    weights(a, b, close and b < 3).wait()

        def some(a, carry):
            ready(a, True)
            for b in range(6):
                visit(a, b, b < 3, bx)
            return carry

        def rest(a, carry):
            ready(a, False)
            for b in range(6):
                visit(a, b, False, bx)
            return carry

        lax.fori_loop(0, 3, some, 0, unroll=3)
        lax.fori_loop(3, 6, rest, 0, unroll=3)

    sweep(0)

    own = back[pl.ds(pl.multiple_of(rep * 32, 32), 32), :]
    arrived = jnp.dot(
        own.astype(F32), nat_i[...], precision=lax.Precision.HIGHEST, preferred_element_type=F32
    )
    present = jnp.dot(own, nat_m[...], preferred_element_type=F32)
    check = 0.5 * jnp.concatenate([acc_c[0], acc_c[1]], axis=0) + arrived
    dense = jnp.dot(check, c2d[...], precision=lax.Precision.HIGHEST, preferred_element_type=F32)
    gath[rep] = (2.0 * dense * present).astype(BF)

    def share(k):
        return pltpu.make_async_remote_copy(
            src_ref=gath.at[rep],
            dst_ref=gath.at[rep],
            send_sem=gs.at[k - 1],
            recv_sem=gr.at[k - 1],
            device_id={"rep": (rep + k) % 4},
            device_id_type=MESH,
        )

    def receive(k):
        return pltpu.make_async_remote_copy(
            src_ref=gath.at[rep],
            dst_ref=gath.at[(rep + 4 - k) % 4],
            send_sem=gs.at[k - 1],
            recv_sem=gr.at[k - 1],
            device_id={"rep": (rep + k) % 4},
            device_id_type=MESH,
        )

    for k in range(1, 4):
        share(k).start()

    sweep(1)

    own_l.wait()
    for k in range(1, 4):
        receive(k).wait_recv()
    parents = jnp.dot(
        order[...], gath[...].reshape(128, COEFFS), preferred_element_type=F32
    ).astype(BF)
    base = pl.multiple_of(((by + 2) * 6 + 2) * 16, 16)
    there = jnp.dot(sel[pl.ds(base, 32), :], mask_f.astype(BF), preferred_element_type=F32)
    for bx in range(2):
        down_part = jnp.dot(parents, l_v[bx, :COEFFS], preferred_element_type=F32)
        dense = jnp.dot(
            acc[bx] + down_part, c2d[...], precision=lax.Precision.HIGHEST, preferred_element_type=F32
        )
        for z in range(8):
            rows = slice(bx * 16, bx * 16 + 16)
            kept = jnp.where(bz == 1, there[rows, 2 * z + 1:2 * z + 2], there[rows, 2 * z:2 * z + 1])
            layer = dense[z * 16:z * 16 + 16] * kept
            for y in range(4):
                out[bx, z, y] = layer[4 * y:4 * y + 4]

    for k in range(1, 4):
        share(k).wait_send()

    @pl.when(has_low)
    def _():
        for copy in down():
            copy.wait_send()

    @pl.when(has_high)
    def _():
        for copy in up():
            copy.wait_send()


def shards(leaves, tables, fm, fp, cm, cp, inc, c2d):
    w, l, sel, selc, order = tables
    operands = (
        fm, fp.transpose(1, 2, 0), cm, cp.transpose(1, 2, 0), inc, c2d,
        sel, selc, order, order.T, w, l,
    )
    vmem = pl.BlockSpec(memory_space=pltpu.VMEM)
    hbm = pl.BlockSpec(memory_space=pltpu.HBM)
    dma = pltpu.SemaphoreType.DMA
    operands = tuple(jnp.asarray(t) for t in operands)
    return pl.pallas_call(
        functools.partial(kernel, leaves),
        out_shape=jax.ShapeDtypeStruct((2, 8, 4, 4, COEFFS), F32),
        in_specs=[hbm] * 12,
        out_specs=vmem,
        scratch_shapes=[pltpu.VMEM(t.shape, t.dtype) for t in operands[:10]]
        + [
            pltpu.VMEM((20, 64, COEFFS), BF),
            pltpu.VMEM((12, 16, COEFFS), BF),
            pltpu.VMEM((36, 2, 160, COEFFS), BF),
            pltpu.VMEM((6, 36, 16, COEFFS), BF),
            pltpu.VMEM((36, 7, DEEP, COEFFS), BF),
            pltpu.VMEM((2, DEEP, COEFFS), BF),
            pltpu.VMEM((2, 128, COEFFS), F32),
            pltpu.VMEM((2, 16, COEFFS), F32),
            pltpu.VMEM((16, 8), F32),
            pltpu.VMEM((128, COEFFS), F32),
            pltpu.VMEM((128, COEFFS), BF),
            pltpu.VMEM((128, COEFFS), F32),
            pltpu.VMEM((4, 32, COEFFS), BF),
            dma((10,)),
            dma((36,)),
            dma,
            dma((4,)),
            dma((4,)),
            dma((3,)),
            dma((3,)),
        ],
        compiler_params=pltpu.CompilerParams(
            collective_id=0, has_side_effects=True, vmem_limit_bytes=63 * 2**20
        ),
    )(*operands)


def solution(mesh):
    leaves = mesh.shape["leaf"]
    tables = (
        translation_table(),
        transfer_table(),
        fine_selection().astype(ml_dtypes.bfloat16),
        coarse_selection().astype(ml_dtypes.bfloat16),
        parent_order().astype(ml_dtypes.bfloat16),
    )
    in_specs = (
        P("leaf", None, None, None),
        P("leaf", None, None),
        P("leaf", None, None, None),
        P("leaf", None, None),
        P("leaf", None, None, None),
        P(),
    )

    def body(*args):
        return shards(leaves, tables, *args)

    out_specs = P("rep", "leaf", None, None, None)
    return jax.shard_map(body, mesh=mesh, in_specs=in_specs, out_specs=out_specs, check_vma=False)
```
